1024 devices in a mesh: group: 16 (over y, core), expert: 64 (over x, z).
Axes of the slice: x: 4, y: 8, z: 16, core: 2. Of those that a mesh axis runs over, the one named last changes fastest.
Arguments:
- tokens: bfloat16 [4096, 4096], P(('group', 'expert')), may hold values from -6 to 6
- expert_ids: int32 [4096, 8], P(('group', 'expert')), may hold values from 0 to 127, as said below
- gates: bfloat16 [4096, 8], P(('group', 'expert')), may hold values from 0.099609375 to 1
- gate_weight: bfloat16 [1024, 4096, 128], P(('group', 'expert')), may hold values from -0.09375 to 0.09375
- up_weight: bfloat16 [1024, 4096, 128], P(('group', 'expert')), may hold values from -0.09375 to 0.09375
- down_weight: bfloat16 [1024, 128, 4096], P(('group', 'expert')), may hold values from -0.1875 to 0.1875
Outputs:
- mixed: bfloat16 [4096, 4096], P(('group', 'expert'))
The draws below stay inside these ranges and needn't reach their ends.
Inputs may be any that keep to these rules, and one draw needn't show every extreme that they name: `expert_ids`: each token names 8 different experts lying in exactly 4 groups, with one to 4 of them in each of those groups. The tokens of one device use any one group at most 1 times, and every device reaches 1 for some group. Among the tokens of the 16 devices that share one index along expert, at most 8 name any one expert, and in every draw some expert is named exactly that often.
All inputs are finite; a program needn't handle non-finite values.
Results may differ from the reference program's by a relative error of at most 0.006.
Values may be sent and summed in bfloat16 or wider, within the bound.
No kernel may reach another device: no remote copies, remote signals or barrier semaphores. Data moves between devices by JAX's collectives and lax.ppermute only.
A program may use at most 32 MiB of HBM per device.

```python
import math
import jax
import jax.numpy as jnp
import numpy as np
from jax import lax

D = 4096
FF = 1024
EXP_GROUP = 8
TOP = 8
TOK_DEV = 4
SLICES = 8
HID = 128
CAP = 8
EXPERTS = 128
TOKENS = 4096
N_GROUP = 16
N_EXPERT = 64


SHARE_TABLE = np.array([[2, 2, 2, 2], [1, 2, 2, 3], [1, 1, 3, 3], [1, 1, 2, 4], [1, 2, 1, 4], [3, 3, 1, 1]], dtype=np.int32)


def permutations(key, count, length):
    return jax.vmap(lambda sub: jax.random.permutation(sub, length))(jax.random.split(key, count)).astype(jnp.int32)


def draw_expert_ids(key, part):
    key = jax.random.fold_in(key, 11)
    keys = jax.random.split(key, 6)
    groups = N_GROUP
    columns = N_EXPERT
    tok_rows = TOK_DEV
    base = permutations(keys[0], columns, groups)
    slot_index = (jnp.arange(tok_rows, dtype=jnp.int32)[:, None] * 4 + jnp.arange(4, dtype=jnp.int32)[None, :]) % groups
    offsets = base[:, slot_index]
    source = jnp.arange(groups, dtype=jnp.int32)[:, None, None, None]
    target = (source + offsets[None]) % groups
    orders = permutations(keys[2], groups * columns, EXP_GROUP).reshape(groups, columns, EXP_GROUP)
    column_index = jnp.arange(columns, dtype=jnp.int32)[None, :, None, None]
    chosen_order = orders[target, column_index]
    shape_five = (groups, columns, tok_rows, 4, 4)
    half_of = (jnp.arange(4, dtype=jnp.int32) % 2)[None, None, None, :, None]
    within = jnp.broadcast_to(half_of * 4 + jnp.arange(4, dtype=jnp.int32)[None, None, None, None, :], shape_five)
    half_set = jnp.take_along_axis(chosen_order, within, axis=4)
    count = groups * columns * tok_rows * 4
    tails = permutations(keys[3], count, 3).reshape(groups, columns, tok_rows, 4, 3) + 1
    leads = jnp.zeros((groups, columns, tok_rows, 4, 1), jnp.int32)
    positions = jnp.concatenate([leads, tails], axis=4)
    picks = jnp.take_along_axis(half_set, positions, axis=4)
    share_index = jax.random.randint(keys[4], (groups, columns, tok_rows), 0, SHARE_TABLE.shape[0], dtype=jnp.int32)
    shares = jnp.asarray(SHARE_TABLE)[share_index]
    rotate = permutations(keys[5], groups * columns * tok_rows, 4).reshape(groups, columns, tok_rows, 4)
    shares = jnp.take_along_axis(shares, rotate, axis=3)
    is_valid = (jnp.arange(4, dtype=jnp.int32)[None, None, None, None, :] < shares[..., None]).astype(jnp.int32)
    full_ids = target[..., None] * EXP_GROUP + picks
    flat_valid = is_valid.reshape(-1, 16)
    flat_ids = full_ids.reshape(-1, 16)
    destination = jnp.cumsum(flat_valid, axis=1) - flat_valid
    landing = (destination[:, :, None] == jnp.arange(TOP, dtype=jnp.int32)[None, None, :]) & (flat_valid[:, :, None] == 1)
    result = jnp.sum(jnp.where(landing, flat_ids[:, :, None], 0), axis=1)
    return result.reshape(TOKENS, TOP).astype(jnp.int32)


def block_scale(stream_key, shape, pieces, least, largest):
    gain = 1.0
    for dim, shards_of in pieces:
        steps = jax.random.uniform(jax.random.fold_in(jax.random.fold_in(stream_key, 6), dim), (shards_of,), jnp.float32, least / len(pieces), largest / len(pieces))
        gain = gain * jnp.repeat(jnp.exp(steps), shape[dim] // shards_of).reshape((-1,) + (1,) * (len(shape) - 1 - dim))
    return gain


def normal_values(rng, dims, spread, most, shards=(), held_as=jnp.bfloat16):
    entries = spread * jax.random.normal(rng, dims, jnp.float32)
    if shards:
        entries = entries * block_scale(rng, dims, shards, -0.22, 0.18)
    return jnp.clip(entries, -most, most).astype(held_as)


def setup_inputs(seed: int = 0) -> dict:
    arg_keys = jax.random.split(jax.random.key(seed), 7)
    tokens = normal_values(arg_keys[0], (TOKENS, D), 1.0, 6.0, ((0, 1024),))
    expert_ids = draw_expert_ids(jax.random.fold_in(arg_keys[6], 71), 0)
    gates = jnp.clip(jnp.exp(math.log(1.0) - 2.306499 * jax.random.uniform(arg_keys[2], (TOKENS, TOP), jnp.float32) ** block_scale(arg_keys[2], (TOKENS, TOP), ((0, 1024),), -0.2, 0.2)), 0.099609375, 1.0).astype(jnp.bfloat16)
    gate_weight = normal_values(arg_keys[3], (EXPERTS * SLICES, D, HID), D ** -0.5, 0.09375, ((0, 1024),))
    up_weight = normal_values(arg_keys[4], (EXPERTS * SLICES, D, HID), D ** -0.5, 0.09375, ((0, 1024),))
    down_weight = normal_values(arg_keys[5], (EXPERTS * SLICES, HID, D), FF ** -0.5, 0.1875, ((0, 1024),))
    return {"tokens": tokens, "expert_ids": expert_ids, "gates": gates, "gate_weight": gate_weight, "up_weight": up_weight, "down_weight": down_weight}


def reference(tokens, expert_ids, gates, gate_weight, up_weight, down_weight):
    flat_ids = expert_ids.reshape(-1).astype(jnp.int32)
    sorted_pairs = jnp.argsort(flat_ids, stable=True).astype(jnp.int32)
    counts = jnp.sum((flat_ids[None, :] == jnp.arange(EXPERTS, dtype=jnp.int32)[:, None]).astype(jnp.int32), axis=1)
    starts = (jnp.cumsum(counts) - counts).astype(jnp.int32)
    capacity = CAP * N_EXPERT
    padded = jnp.concatenate([sorted_pairs, jnp.zeros((capacity,), jnp.int32)])
    flat_gates = gates.reshape(-1)

    def one_expert(running, expert):
        pair_ids = lax.dynamic_slice_in_dim(padded, starts[expert], capacity)
        is_live = jnp.arange(capacity, dtype=jnp.int32) < counts[expert]
        token_index = (pair_ids // TOP).astype(jnp.int32)
        token_rows = tokens[token_index]
        pair_gate = jnp.where(is_live, flat_gates[pair_ids].astype(jnp.float32), jnp.float32(0.0))
        summed = jnp.zeros((capacity, D), jnp.float32)
        for slice_index in range(SLICES):
            weight_row = expert * SLICES + slice_index
            w_gate = lax.dynamic_index_in_dim(gate_weight, weight_row, 0, keepdims=False)
            w_up = lax.dynamic_index_in_dim(up_weight, weight_row, 0, keepdims=False)
            w_down = lax.dynamic_index_in_dim(down_weight, weight_row, 0, keepdims=False)
            gate_act = jnp.dot(token_rows, w_gate, preferred_element_type=jnp.float32)
            up_act = jnp.dot(token_rows, w_up, preferred_element_type=jnp.float32)
            hidden = (jax.nn.silu(gate_act) * up_act).astype(jnp.bfloat16)
            partial_rows = jnp.dot(hidden, w_down, preferred_element_type=jnp.float32).astype(jnp.bfloat16)
            summed = summed + partial_rows.astype(jnp.float32)
        running = running.at[token_index].add(pair_gate[:, None] * summed)
        return running, None

    running, _ = lax.scan(one_expert, jnp.zeros((TOKENS, D), jnp.float32), jnp.arange(EXPERTS, dtype=jnp.int32))
    return running.astype(jnp.bfloat16)
```

```python
import jax
import jax.numpy as jnp
from jax import lax
from jax.sharding import Mesh, PartitionSpec as P

EXP_GROUP = 8
LANES = 128
X_CHIPS = 4
FRONT = 2048


def on_device(tokens, expert_ids, gates, gate_weight, up_weight, down_weight):
    groups = lax.axis_size("group")
    nx = lax.axis_size("x")
    nz = lax.axis_size("z")
    slices = nx * nz // EXP_GROUP
    features = tokens.shape[1]
    units = gate_weight.shape[2]
    x_me = lax.axis_index("x")
    to_right = [(i, (i + 1) % nx) for i in range(nx)]
    to_left = [(i, (i - 1) % nx) for i in range(nx)]

    group_of = expert_ids // EXP_GROUP
    local_of = expert_ids % EXP_GROUP
    group_hit = (
        group_of[:, :, None] == jnp.arange(groups, dtype=jnp.int32)[None, None, :]
    ).astype(jnp.float32)
    local_hit = (
        local_of[:, :, None] == jnp.arange(EXP_GROUP, dtype=jnp.int32)[None, None, :]
    ).astype(jnp.float32)
    chosen = (jnp.sum(group_hit, axis=1) > 0).astype(jnp.bfloat16)
    send_rows = jnp.einsum(
        "tg,td->gd", chosen, tokens, preferred_element_type=jnp.float32
    ).astype(jnp.bfloat16)
    weighted_hit = local_hit * gates.astype(jnp.float32)[:, :, None]
    gate_table = jnp.sum(
        group_hit[:, :, :, None] * weighted_hit[:, :, None, :], axis=(0, 1)
    ).astype(jnp.bfloat16)
    packed = jnp.concatenate(
        [
            send_rows[:, :FRONT],
            jnp.pad(gate_table, ((0, 0), (0, LANES - EXP_GROUP))),
            send_rows[:, FRONT:],
        ],
        axis=1,
    )
    arrived = lax.all_to_all(packed, "group", split_axis=0, concat_axis=0, tiled=True)
    front = arrived[:, : FRONT + LANES]
    back = arrived[:, FRONT + LANES :]
    back_width = features - FRONT
    half = back_width // 2

    back_own = lax.all_gather(back, "z", axis=0, tiled=True)
    front_x = lax.all_gather(front, "x", axis=0, tiled=True)
    front_all = lax.all_gather(front_x, "z", axis=0, tiled=True)
    back_left = lax.ppermute(back_own, "x", to_right)
    back_right = lax.ppermute(back_own, "x", to_left)
    far_low = lax.ppermute(back_left[:, :half], "x", to_right)
    far_high = lax.ppermute(back_right[:, half:], "x", to_left)

    both = jnp.concatenate([gate_weight[0], up_weight[0]], axis=1)
    both_front, both_back = both[:FRONT], both[FRONT:]

    def dot(a, b):
        return jnp.dot(a, b, preferred_element_type=jnp.float32)

    rows_z = back_own.shape[0]
    by_offset = jnp.stack(
        [
            dot(back_own, both_back),
            dot(back_right, both_back),
            dot(far_low, both_back[:half]) + dot(far_high, both_back[half:]),
            dot(back_left, both_back),
        ]
    ).reshape(nx, nz, groups, 2 * units)
    act_back = jnp.stack(
        [
            lax.dynamic_index_in_dim(by_offset, (x - x_me + nx) % nx, 0, keepdims=False)
            for x in range(nx)
        ],
        axis=1,
    ).reshape(nz * nx * groups, 2 * units)
    act = dot(front_all[:, :FRONT], both_front) + act_back
    hidden = (jax.nn.silu(act[:, :units]) * act[:, units:]).astype(jnp.bfloat16)
    mine = (x_me * nz + lax.axis_index("z")) // slices
    own = (jnp.arange(LANES, dtype=jnp.int32) == mine).astype(jnp.float32)
    scale = jnp.sum(front_all[:, FRONT:].astype(jnp.float32) * own[None, :], axis=1, keepdims=True)

    down = down_weight[0]
    front_out = (dot(hidden, down[:, :FRONT]) * scale).astype(jnp.bfloat16)
    front_z = lax.psum_scatter(front_out, "z", scatter_dimension=0, tiled=True)
    front_parts = lax.all_to_all(front_z, "x", split_axis=0, concat_axis=0, tiled=True)
    front_sum = jnp.sum(
        front_parts.reshape(nx, groups, FRONT), axis=0, dtype=jnp.float32
    ).astype(jnp.bfloat16)

    down_low, down_high = down[:, FRONT : FRONT + half], down[:, FRONT + half :]
    hidden_x = hidden.reshape(nz, nx, groups, units)
    scale_x = scale.reshape(nz, nx, groups, 1)

    def block(offset):
        at = (x_me + offset) % nx
        return (
            lax.dynamic_index_in_dim(hidden_x, at, 1, keepdims=False).reshape(rows_z, units),
            lax.dynamic_index_in_dim(scale_x, at, 1, keepdims=False).reshape(rows_z, 1),
        )

    h_far, s_far = block(2)
    h_right, s_right = block(1)
    h_left, s_left = block(3)
    h_own, s_own = block(0)
    low_in = lax.ppermute((dot(h_far, down_low) * s_far).astype(jnp.bfloat16), "x", to_right)
    high_in = lax.ppermute((dot(h_far, down_high) * s_far).astype(jnp.bfloat16), "x", to_left)
    send_right = jnp.concatenate(
        [dot(h_right, down_low) * s_right + low_in, dot(h_right, down_high) * s_right], axis=1
    ).astype(jnp.bfloat16)
    send_left = jnp.concatenate(
        [dot(h_left, down_low) * s_left, dot(h_left, down_high) * s_left + high_in], axis=1
    ).astype(jnp.bfloat16)
    from_left = lax.ppermute(send_right, "x", to_right)
    from_right = lax.ppermute(send_left, "x", to_left)
    back_out = (dot(h_own, down[:, FRONT:]) * s_own + from_left + from_right).astype(jnp.bfloat16)
    back_sum = lax.psum_scatter(back_out, "z", scatter_dimension=0, tiled=True)

    home = lax.all_to_all(
        jnp.concatenate([front_sum, back_sum], axis=1),
        "group",
        split_axis=0,
        concat_axis=0,
        tiled=True,
    )
    result = jnp.einsum("tg,gd->td", chosen, home, preferred_element_type=jnp.float32)
    return result.astype(jnp.bfloat16)


def solution(mesh):
    groups, columns = mesh.devices.shape
    fine = Mesh(
        mesh.devices.reshape(groups, X_CHIPS, columns // X_CHIPS), ("group", "x", "z")
    )
    lead = ("group", "x", "z")
    in_specs = (
        P(lead, None),
        P(lead, None),
        P(lead, None),
        P(lead, None, None),
        P(lead, None, None),
        P(lead, None, None),
    )
    return jax.shard_map(
        on_device, mesh=fine, in_specs=in_specs, out_specs=P(lead, None), check_vma=False
    )
```

```python
import jax
import jax.numpy as jnp
from jax import lax
from jax.sharding import Mesh, PartitionSpec as P

EXP_GROUP = 8
LANES = 128
X_CHIPS = 4
FRONT = 3072


def on_device(tokens, expert_ids, gates, gate_weight, up_weight, down_weight):
    groups = lax.axis_size("group")
    nx = lax.axis_size("x")
    nz = lax.axis_size("z")
    slices = nx * nz // EXP_GROUP
    features = tokens.shape[1]
    units = gate_weight.shape[2]
    x_me = lax.axis_index("x")
    to_right = [(i, (i + 1) % nx) for i in range(nx)]
    to_left = [(i, (i - 1) % nx) for i in range(nx)]

    group_of = expert_ids // EXP_GROUP
    local_of = expert_ids % EXP_GROUP
    group_hit = (
        group_of[:, :, None] == jnp.arange(groups, dtype=jnp.int32)[None, None, :]
    ).astype(jnp.float32)
    local_hit = (
        local_of[:, :, None] == jnp.arange(EXP_GROUP, dtype=jnp.int32)[None, None, :]
    ).astype(jnp.float32)
    chosen = (jnp.sum(group_hit, axis=1) > 0).astype(jnp.bfloat16)
    send_rows = jnp.einsum(
        "tg,td->gd", chosen, tokens, preferred_element_type=jnp.float32
    ).astype(jnp.bfloat16)
    weighted_hit = local_hit * gates.astype(jnp.float32)[:, :, None]
    gate_table = jnp.sum(
        group_hit[:, :, :, None] * weighted_hit[:, :, None, :], axis=(0, 1)
    ).astype(jnp.bfloat16)
    width = features - FRONT
    half = width // 2
    front_row = jnp.concatenate(
        [send_rows[:, :FRONT], jnp.pad(gate_table, ((0, 0), (0, LANES - EXP_GROUP)))], axis=1
    )

    front = lax.all_to_all(
        jnp.broadcast_to(front_row[:, None], (groups, nx, FRONT + LANES)).reshape(
            groups * nx, FRONT + LANES
        ),
        ("group", "x"),
        split_axis=0,
        concat_axis=0,
        tiled=True,
    )
    front_all = lax.all_gather(front, "z", axis=0, tiled=True)
    back_row, _ = lax.optimization_barrier((send_rows[:, FRONT:], front))
    back = lax.all_to_all(back_row, "group", split_axis=0, concat_axis=0, tiled=True)
    back_own = lax.all_gather(back, "z", axis=0, tiled=True)
    back_left = lax.ppermute(back_own, "x", to_right)
    back_right = lax.ppermute(back_own, "x", to_left)
    far_low = lax.ppermute(back_left[:, :half], "x", to_right)
    far_high = lax.ppermute(back_right[:, half:], "x", to_left)

    both = jnp.concatenate([gate_weight[0], up_weight[0]], axis=1)
    both_front, both_back = both[:FRONT], both[FRONT:]

    def dot(a, b):
        return jnp.dot(a, b, preferred_element_type=jnp.float32)

    rows_z = back_own.shape[0]
    by_offset = jnp.stack(
        [
            dot(back_own, both_back),
            dot(back_right, both_back),
            dot(far_low, both_back[:half]) + dot(far_high, both_back[half:]),
            dot(back_left, both_back),
        ]
    ).reshape(nx, nz, groups, 2 * units)
    act_back = jnp.stack(
        [
            lax.dynamic_index_in_dim(by_offset, (x - x_me + nx) % nx, 0, keepdims=False)
            for x in range(nx)
        ],
        axis=2,
    ).reshape(nz * groups * nx, 2 * units)
    act = dot(front_all[:, :FRONT], both_front) + act_back
    hidden = (jax.nn.silu(act[:, :units]) * act[:, units:]).astype(jnp.bfloat16)
    mine = (x_me * nz + lax.axis_index("z")) // slices
    own = (jnp.arange(LANES, dtype=jnp.int32) == mine).astype(jnp.float32)
    scale = jnp.sum(front_all[:, FRONT:].astype(jnp.float32) * own[None, :], axis=1, keepdims=True)

    down = down_weight[0]
    front_out = (dot(hidden, down[:, :FRONT]) * scale).astype(jnp.bfloat16)
    front_z = lax.psum_scatter(front_out, "z", scatter_dimension=0, tiled=True)
    down_low, down_high = down[:, FRONT : FRONT + half], down[:, FRONT + half :]
    hidden_x = hidden.reshape(nz, groups, nx, units)
    scale_x = scale.reshape(nz, groups, nx, 1)

    def block(offset):
        at = (x_me + offset) % nx
        return (
            lax.dynamic_index_in_dim(hidden_x, at, 2, keepdims=False).reshape(rows_z, units),
            lax.dynamic_index_in_dim(scale_x, at, 2, keepdims=False).reshape(rows_z, 1),
        )

    h_far, s_far = block(2)
    h_right, s_right = block(1)
    h_left, s_left = block(3)
    h_own, s_own = block(0)
    low_in = lax.ppermute((dot(h_far, down_low) * s_far).astype(jnp.bfloat16), "x", to_right)
    high_in = lax.ppermute((dot(h_far, down_high) * s_far).astype(jnp.bfloat16), "x", to_left)
    send_right = jnp.concatenate(
        [dot(h_right, down_low) * s_right + low_in, dot(h_right, down_high) * s_right], axis=1
    ).astype(jnp.bfloat16)
    send_left = jnp.concatenate(
        [dot(h_left, down_low) * s_left, dot(h_left, down_high) * s_left + high_in], axis=1
    ).astype(jnp.bfloat16)
    from_left = lax.ppermute(send_right, "x", to_right)
    from_right = lax.ppermute(send_left, "x", to_left)
    back_out = (dot(h_own, down[:, FRONT:]) * s_own + from_left + from_right).astype(jnp.bfloat16)
    back_parts = lax.all_to_all(back_out, "z", split_axis=0, concat_axis=0, tiled=True)
    back_sum = jnp.sum(
        back_parts.reshape(nz, groups, width), axis=0, dtype=jnp.float32
    ).astype(jnp.bfloat16)
    back_home = lax.all_to_all(back_sum, "group", split_axis=0, concat_axis=0, tiled=True)
    front_home = lax.all_to_all(
        front_z, ("group", "x"), split_axis=0, concat_axis=0, tiled=True
    )
    result = jnp.concatenate(
        [dot(jnp.repeat(chosen, nx, axis=1), front_home), dot(chosen, back_home)], axis=1
    )
    return result.astype(jnp.bfloat16)


def solution(mesh):
    groups, columns = mesh.devices.shape
    fine = Mesh(
        mesh.devices.reshape(groups, X_CHIPS, columns // X_CHIPS), ("group", "x", "z")
    )
    lead = ("group", "x", "z")
    in_specs = (
        P(lead, None),
        P(lead, None),
        P(lead, None),
        P(lead, None, None),
        P(lead, None, None),
        P(lead, None, None),
    )
    return jax.shard_map(
        on_device, mesh=fine, in_specs=in_specs, out_specs=P(lead, None), check_vma=False
    )
```

```python
import jax
import jax.numpy as jnp
from jax import lax
from jax.sharding import Mesh, PartitionSpec as P

EXP_GROUP = 8
LANES = 128
X_CHIPS = 4
FRONT = 2304


def on_device(tokens, expert_ids, gates, gate_weight, up_weight, down_weight):
    groups = lax.axis_size("group")
    nx = lax.axis_size("x")
    nz = lax.axis_size("z")
    slices = nx * nz // EXP_GROUP
    features = tokens.shape[1]
    units = gate_weight.shape[2]
    x_me = lax.axis_index("x")
    to_right = [(i, (i + 1) % nx) for i in range(nx)]
    to_left = [(i, (i - 1) % nx) for i in range(nx)]

    group_of = expert_ids // EXP_GROUP
    local_of = expert_ids % EXP_GROUP
    group_hit = (
        group_of[:, :, None] == jnp.arange(groups, dtype=jnp.int32)[None, None, :]
    ).astype(jnp.float32)
    local_hit = (
        local_of[:, :, None] == jnp.arange(EXP_GROUP, dtype=jnp.int32)[None, None, :]
    ).astype(jnp.float32)
    chosen = (jnp.sum(group_hit, axis=1) > 0).astype(jnp.bfloat16)
    send_rows = jnp.einsum(
        "tg,td->gd", chosen, tokens, preferred_element_type=jnp.float32
    ).astype(jnp.bfloat16)
    weighted_hit = local_hit * gates.astype(jnp.float32)[:, :, None]
    gate_table = jnp.sum(
        group_hit[:, :, :, None] * weighted_hit[:, :, None, :], axis=(0, 1)
    ).astype(jnp.bfloat16)
    width = features - FRONT
    half = width // 2
    front_row = jnp.concatenate(
        [send_rows[:, :FRONT], jnp.pad(gate_table, ((0, 0), (0, LANES - EXP_GROUP)))], axis=1
    )

    front = lax.all_to_all(
        jnp.broadcast_to(front_row[:, None], (groups, nx, FRONT + LANES)).reshape(
            groups * nx, FRONT + LANES
        ),
        ("group", "x"),
        split_axis=0,
        concat_axis=0,
        tiled=True,
    )
    front_all = lax.all_gather(front, "z", axis=0, tiled=True)
    back_row = jnp.concatenate(
        [tokens[:, FRONT:], jnp.pad(chosen, ((0, 0), (0, LANES - groups)))], axis=1
    )
    back_row, _ = lax.optimization_barrier((back_row, front))
    column = lax.all_gather(back_row, "z", axis=0, tiled=True)
    tok_rows = tokens.shape[0]
    same_z = (
        jnp.arange(nz, dtype=jnp.int32)[:, None]
        == jnp.arange(nz * tok_rows, dtype=jnp.int32)[None, :] // tok_rows
    ).astype(jnp.bfloat16)
    place = (column[:, width : width + groups].T[:, None, :] * same_z[None]).reshape(
        groups * nz, nz * tok_rows
    )
    back = jnp.dot(place, column[:, :width], preferred_element_type=jnp.float32).astype(
        jnp.bfloat16
    )
    back_own = lax.all_to_all(back, "group", split_axis=0, concat_axis=0, tiled=True)
    back_left = lax.ppermute(back_own, "x", to_right)
    back_right = lax.ppermute(back_own, "x", to_left)
    far_low = lax.ppermute(back_left[:, :half], "x", to_right)
    far_high = lax.ppermute(back_right[:, half:], "x", to_left)

    both = jnp.concatenate([gate_weight[0], up_weight[0]], axis=1)
    both_front, both_back = both[:FRONT], both[FRONT:]

    def dot(a, b):
        return jnp.dot(a, b, preferred_element_type=jnp.float32)

    rows_z = back_own.shape[0]
    by_offset = jnp.stack(
        [
            dot(back_own, both_back),
            dot(back_right, both_back),
            dot(far_low, both_back[:half]) + dot(far_high, both_back[half:]),
            dot(back_left, both_back),
        ]
    ).reshape(nx, groups, nz, 2 * units)
    act_back = jnp.stack(
        [
            lax.dynamic_index_in_dim(by_offset, (x - x_me + nx) % nx, 0, keepdims=False)
            for x in range(nx)
        ],
        axis=2,
    ).transpose(1, 0, 2, 3).reshape(nz * groups * nx, 2 * units)
    act = dot(front_all[:, :FRONT], both_front) + act_back
    hidden = (jax.nn.silu(act[:, :units]) * act[:, units:]).astype(jnp.bfloat16)
    mine = (x_me * nz + lax.axis_index("z")) // slices
    own = (jnp.arange(LANES, dtype=jnp.int32) == mine).astype(jnp.float32)
    scale = jnp.sum(front_all[:, FRONT:].astype(jnp.float32) * own[None, :], axis=1, keepdims=True)

    down = down_weight[0]
    front_out = (dot(hidden, down[:, :FRONT]) * scale).astype(jnp.bfloat16)
    front_z = lax.psum_scatter(front_out, "z", scatter_dimension=0, tiled=True)
    down_low, down_high = down[:, FRONT : FRONT + half], down[:, FRONT + half :]
    hidden_x = hidden.reshape(nz, groups, nx, units)
    scale_x = scale.reshape(nz, groups, nx, 1)

    def block(offset):
        at = (x_me + offset) % nx
        return (
            lax.dynamic_index_in_dim(hidden_x, at, 2, keepdims=False).swapaxes(0, 1).reshape(rows_z, units),
            lax.dynamic_index_in_dim(scale_x, at, 2, keepdims=False).swapaxes(0, 1).reshape(rows_z, 1),
        )

    h_far, s_far = block(2)
    h_right, s_right = block(1)
    h_left, s_left = block(3)
    h_own, s_own = block(0)
    low_in = lax.ppermute((dot(h_far, down_low) * s_far).astype(jnp.bfloat16), "x", to_right)
    high_in = lax.ppermute((dot(h_far, down_high) * s_far).astype(jnp.bfloat16), "x", to_left)
    send_right = jnp.concatenate(
        [dot(h_right, down_low) * s_right + low_in, dot(h_right, down_high) * s_right], axis=1
    ).astype(jnp.bfloat16)
    send_left = jnp.concatenate(
        [dot(h_left, down_low) * s_left, dot(h_left, down_high) * s_left + high_in], axis=1
    ).astype(jnp.bfloat16)
    from_left = lax.ppermute(send_right, "x", to_right)
    from_right = lax.ppermute(send_left, "x", to_left)
    back_out = (dot(h_own, down[:, FRONT:]) * s_own + from_left + from_right).astype(jnp.bfloat16)
    back_group = lax.all_to_all(back_out, "group", split_axis=0, concat_axis=0, tiled=True)
    back_tokens = jnp.einsum(
        "rt,rd->td", place, back_group, preferred_element_type=jnp.float32
    ).astype(jnp.bfloat16)
    back_parts = lax.all_to_all(back_tokens, "z", split_axis=0, concat_axis=0, tiled=True)
    back_home = jnp.sum(back_parts.reshape(nz, tok_rows, width), axis=0, dtype=jnp.float32)
    front_home = lax.all_to_all(
        front_z, ("group", "x"), split_axis=0, concat_axis=0, tiled=True
    )
    result = jnp.concatenate(
        [dot(jnp.repeat(chosen, nx, axis=1), front_home), back_home], axis=1
    )
    return result.astype(jnp.bfloat16)


def solution(mesh):
    groups, columns = mesh.devices.shape
    fine = Mesh(
        mesh.devices.reshape(groups, X_CHIPS, columns // X_CHIPS), ("group", "x", "z")
    )
    lead = ("group", "x", "z")
    in_specs = (
        P(lead, None),
        P(lead, None),
        P(lead, None),
        P(lead, None, None),
        P(lead, None, None),
        P(lead, None, None),
    )
    return jax.shard_map(
        on_device, mesh=fine, in_specs=in_specs, out_specs=P(lead, None), check_vma=False
    )
```

```python
import jax
import jax.numpy as jnp
from jax import lax
from jax.sharding import Mesh, PartitionSpec as P

EXP_GROUP = 8
LANES = 128
X_CHIPS = 4
FRONT = 2048
FRONT_OUT = 2560


def on_device(tokens, expert_ids, gates, gate_weight, up_weight, down_weight):
    groups = lax.axis_size("group")
    nx = lax.axis_size("x")
    nz = lax.axis_size("z")
    slices = nx * nz // EXP_GROUP
    features = tokens.shape[1]
    units = gate_weight.shape[2]
    x_me = lax.axis_index("x")
    to_right = [(i, (i + 1) % nx) for i in range(nx)]
    to_left = [(i, (i - 1) % nx) for i in range(nx)]

    group_of = expert_ids // EXP_GROUP
    local_of = expert_ids % EXP_GROUP
    group_hit = (
        group_of[:, :, None] == jnp.arange(groups, dtype=jnp.int32)[None, None, :]
    ).astype(jnp.float32)
    local_hit = (
        local_of[:, :, None] == jnp.arange(EXP_GROUP, dtype=jnp.int32)[None, None, :]
    ).astype(jnp.float32)
    chosen = (jnp.sum(group_hit, axis=1) > 0).astype(jnp.bfloat16)
    send_rows = jnp.einsum(
        "tg,td->gd", chosen, tokens, preferred_element_type=jnp.float32
    ).astype(jnp.bfloat16)
    weighted_hit = local_hit * gates.astype(jnp.float32)[:, :, None]
    gate_table = jnp.sum(
        group_hit[:, :, :, None] * weighted_hit[:, :, None, :], axis=(0, 1)
    ).astype(jnp.bfloat16)
    width = features - FRONT
    half = width // 2
    front_row = jnp.concatenate(
        [send_rows[:, :FRONT], jnp.pad(gate_table, ((0, 0), (0, LANES - EXP_GROUP)))], axis=1
    )

    back_row = jnp.concatenate(
        [tokens[:, FRONT:], jnp.pad(chosen, ((0, 0), (0, LANES - groups)))], axis=1
    )
    front_send = jnp.broadcast_to(front_row[:, None], (groups, nx, FRONT + LANES)).reshape(
        groups * nx, FRONT + LANES
    )
    back_row, front_send = lax.optimization_barrier((back_row, front_send))
    column = lax.all_gather(back_row, "z", axis=0, tiled=True)
    front = lax.all_to_all(
        front_send,
        ("group", "x"),
        split_axis=0,
        concat_axis=0,
        tiled=True,
    )
    front, column = lax.optimization_barrier((front, column))
    front_all = lax.all_gather(front, "z", axis=0, tiled=True)
    tok_rows = tokens.shape[0]
    same_z = (
        jnp.arange(nz, dtype=jnp.int32)[:, None]
        == jnp.arange(nz * tok_rows, dtype=jnp.int32)[None, :] // tok_rows
    ).astype(jnp.bfloat16)
    place = (column[:, width : width + groups].T[:, None, :] * same_z[None]).reshape(
        groups * nz, nz * tok_rows
    )
    back = jnp.dot(place, column[:, :width], preferred_element_type=jnp.float32).astype(
        jnp.bfloat16
    )
    back_own = lax.all_to_all(back, "group", split_axis=0, concat_axis=0, tiled=True)
    own_low, own_high = back_own[:, :half], back_own[:, half:]
    left_low = lax.ppermute(own_low, "x", to_right)
    right_high = lax.ppermute(own_high, "x", to_left)
    left_high = lax.ppermute(own_high, "x", to_right)
    right_low = lax.ppermute(own_low, "x", to_left)
    far_low = lax.ppermute(left_low, "x", to_right)
    far_high = lax.ppermute(right_high, "x", to_left)

    both = jnp.concatenate([gate_weight[0], up_weight[0]], axis=1)
    both_front, both_back = both[:FRONT], both[FRONT:]
    back_low, back_high = both_back[:half], both_back[half:]

    def dot(a, b):
        return jnp.dot(a, b, preferred_element_type=jnp.float32)

    rows_z = back_own.shape[0]
    by_offset = jnp.stack(
        [
            dot(back_own, both_back),
            dot(right_low, back_low) + dot(right_high, back_high),
            dot(far_low, back_low) + dot(far_high, back_high),
            dot(left_low, back_low) + dot(left_high, back_high),
        ]
    ).reshape(nx, groups, nz, 2 * units)
    act_back = jnp.stack(
        [
            lax.dynamic_index_in_dim(by_offset, (x - x_me + nx) % nx, 0, keepdims=False)
            for x in range(nx)
        ],
        axis=2,
    ).transpose(1, 0, 2, 3).reshape(nz * groups * nx, 2 * units)
    act = dot(front_all[:, :FRONT], both_front) + act_back
    hidden = (jax.nn.silu(act[:, :units]) * act[:, units:]).astype(jnp.bfloat16)
    mine = (x_me * nz + lax.axis_index("z")) // slices
    own = (jnp.arange(LANES, dtype=jnp.int32) == mine).astype(jnp.float32)
    scale = jnp.sum(front_all[:, FRONT:].astype(jnp.float32) * own[None, :], axis=1, keepdims=True)

    down = down_weight[0]
    front_out = (dot(hidden, down[:, :FRONT_OUT]) * scale).astype(jnp.bfloat16)
    front_z = lax.psum_scatter(front_out, "z", scatter_dimension=0, tiled=True)
    out_width = features - FRONT_OUT
    middle = FRONT_OUT + out_width // 2
    down_low, down_high = down[:, FRONT_OUT:middle], down[:, middle:]
    hidden_x = hidden.reshape(nz, groups, nx, units)
    scale_x = scale.reshape(nz, groups, nx, 1)

    def block(offset):
        at = (x_me + offset) % nx
        return (
            lax.dynamic_index_in_dim(hidden_x, at, 2, keepdims=False).swapaxes(0, 1).reshape(rows_z, units),
            lax.dynamic_index_in_dim(scale_x, at, 2, keepdims=False).swapaxes(0, 1).reshape(rows_z, 1),
        )

    h_far, s_far = block(2)
    h_right, s_right = block(1)
    h_left, s_left = block(3)
    h_own, s_own = block(0)

    def part(h, s, weights, more=0.0):
        return (dot(h, weights) * s + more).astype(jnp.bfloat16)

    low_in = lax.ppermute(part(h_far, s_far, down_low), "x", to_right)
    high_in = lax.ppermute(part(h_far, s_far, down_high), "x", to_left)
    left_high_in = lax.ppermute(part(h_right, s_right, down_high), "x", to_right)
    right_low_in = lax.ppermute(part(h_left, s_left, down_low), "x", to_left)
    left_low_in = lax.ppermute(part(h_right, s_right, down_low, low_in), "x", to_right)
    right_high_in = lax.ppermute(part(h_left, s_left, down_high, high_in), "x", to_left)
    back_out = jnp.concatenate(
        [
            part(h_own, s_own, down_low, left_low_in.astype(jnp.float32) + right_low_in),
            part(h_own, s_own, down_high, left_high_in.astype(jnp.float32) + right_high_in),
        ],
        axis=1,
    )
    back_group = lax.all_to_all(back_out, "group", split_axis=0, concat_axis=0, tiled=True)
    back_tokens = jnp.einsum(
        "rt,rd->td", place, back_group, preferred_element_type=jnp.float32
    ).astype(jnp.bfloat16)
    back_parts = lax.all_to_all(back_tokens, "z", split_axis=0, concat_axis=0, tiled=True)
    back_home = jnp.sum(back_parts.reshape(nz, tok_rows, out_width), axis=0, dtype=jnp.float32)
    front_home = lax.all_to_all(
        front_z, ("group", "x"), split_axis=0, concat_axis=0, tiled=True
    )
    result = jnp.concatenate(
        [dot(jnp.repeat(chosen, nx, axis=1), front_home), back_home], axis=1
    )
    return result.astype(jnp.bfloat16)


def solution(mesh):
    groups, columns = mesh.devices.shape
    fine = Mesh(
        mesh.devices.reshape(groups, X_CHIPS, columns // X_CHIPS), ("group", "x", "z")
    )
    lead = ("group", "x", "z")
    in_specs = (
        P(lead, None),
        P(lead, None),
        P(lead, None),
        P(lead, None, None),
        P(lead, None, None),
        P(lead, None, None),
    )
    return jax.shard_map(
        on_device, mesh=fine, in_specs=in_specs, out_specs=P(lead, None), check_vma=False
    )
```

```python
import jax
import jax.numpy as jnp
from jax import lax
from jax.sharding import Mesh, PartitionSpec as P

EXP_GROUP = 8
LANES = 128
X_CHIPS = 4
FRONT = 2560
FRONT_OUT = 2816


def on_device(tokens, expert_ids, gates, gate_weight, up_weight, down_weight):
    groups = lax.axis_size("group")
    nx = lax.axis_size("x")
    nz = lax.axis_size("z")
    slices = nx * nz // EXP_GROUP
    features = tokens.shape[1]
    units = gate_weight.shape[2]
    x_me = lax.axis_index("x")
    to_right = [(i, (i + 1) % nx) for i in range(nx)]
    to_left = [(i, (i - 1) % nx) for i in range(nx)]

    group_of = expert_ids // EXP_GROUP
    local_of = expert_ids % EXP_GROUP
    group_hit = (
        group_of[:, :, None] == jnp.arange(groups, dtype=jnp.int32)[None, None, :]
    ).astype(jnp.float32)
    local_hit = (
        local_of[:, :, None] == jnp.arange(EXP_GROUP, dtype=jnp.int32)[None, None, :]
    ).astype(jnp.float32)
    chosen = (jnp.sum(group_hit, axis=1) > 0).astype(jnp.bfloat16)
    send_rows = jnp.einsum(
        "tg,td->gd", chosen, tokens, preferred_element_type=jnp.float32
    ).astype(jnp.bfloat16)
    weighted_hit = local_hit * gates.astype(jnp.float32)[:, :, None]
    gate_table = jnp.sum(
        group_hit[:, :, :, None] * weighted_hit[:, :, None, :], axis=(0, 1)
    ).astype(jnp.bfloat16)
    width = features - FRONT
    half = width // 2
    front_row = jnp.concatenate(
        [send_rows[:, :FRONT], jnp.pad(gate_table, ((0, 0), (0, LANES - EXP_GROUP)))], axis=1
    )

    back_row = jnp.concatenate(
        [tokens[:, FRONT:], jnp.pad(chosen, ((0, 0), (0, LANES - groups)))], axis=1
    )
    front_send = jnp.broadcast_to(front_row[:, None], (groups, nx, FRONT + LANES)).reshape(
        groups * nx, FRONT + LANES
    )
    back_row, front_send = lax.optimization_barrier((back_row, front_send))
    copies = jnp.broadcast_to(back_row[None], (nz,) + back_row.shape).reshape(
        nz * back_row.shape[0], back_row.shape[1]
    )
    column = lax.all_to_all(copies, "z", split_axis=0, concat_axis=0, tiled=True)
    front = lax.all_to_all(
        front_send,
        ("group", "x"),
        split_axis=0,
        concat_axis=0,
        tiled=True,
    )
    front_all = lax.all_gather(front, "z", axis=0, tiled=True)
    tok_rows = tokens.shape[0]
    same_z = (
        jnp.arange(nz, dtype=jnp.int32)[:, None]
        == jnp.arange(nz * tok_rows, dtype=jnp.int32)[None, :] // tok_rows
    ).astype(jnp.bfloat16)
    place = (column[:, width : width + groups].T[:, None, :] * same_z[None]).reshape(
        groups * nz, nz * tok_rows
    )
    back = jnp.dot(place, column[:, :width], preferred_element_type=jnp.float32).astype(
        jnp.bfloat16
    )
    back_own = lax.all_to_all(back, "group", split_axis=0, concat_axis=0, tiled=True)
    own_low, own_high = back_own[:, :half], back_own[:, half:]
    left_low = lax.ppermute(own_low, "x", to_right)
    right_high = lax.ppermute(own_high, "x", to_left)
    left_high = lax.ppermute(own_high, "x", to_right)
    right_low = lax.ppermute(own_low, "x", to_left)
    far_low = lax.ppermute(left_low, "x", to_right)
    far_high = lax.ppermute(right_high, "x", to_left)

    both = jnp.concatenate([gate_weight[0], up_weight[0]], axis=1)
    both_front, both_back = both[:FRONT], both[FRONT:]
    back_low, back_high = both_back[:half], both_back[half:]

    def dot(a, b):
        return jnp.dot(a, b, preferred_element_type=jnp.float32)

    rows_z = back_own.shape[0]
    by_offset = jnp.stack(
        [
            dot(back_own, both_back),
            dot(right_low, back_low) + dot(right_high, back_high),
            dot(far_low, back_low) + dot(far_high, back_high),
            dot(left_low, back_low) + dot(left_high, back_high),
        ]
    ).reshape(nx, groups, nz, 2 * units)
    act_back = jnp.stack(
        [
            lax.dynamic_index_in_dim(by_offset, (x - x_me + nx) % nx, 0, keepdims=False)
            for x in range(nx)
        ],
        axis=2,
    ).transpose(1, 0, 2, 3).reshape(nz * groups * nx, 2 * units)
    act = dot(front_all[:, :FRONT], both_front) + act_back
    hidden = (jax.nn.silu(act[:, :units]) * act[:, units:]).astype(jnp.bfloat16)
    mine = (x_me * nz + lax.axis_index("z")) // slices
    own = (jnp.arange(LANES, dtype=jnp.int32) == mine).astype(jnp.float32)
    scale = jnp.sum(front_all[:, FRONT:].astype(jnp.float32) * own[None, :], axis=1, keepdims=True)

    down = down_weight[0]
    front_out = (dot(hidden, down[:, :FRONT_OUT]) * scale).astype(jnp.bfloat16)
    front_z = lax.psum_scatter(front_out, "z", scatter_dimension=0, tiled=True)
    out_width = features - FRONT_OUT
    middle = FRONT_OUT + out_width // 2
    down_low, down_high = down[:, FRONT_OUT:middle], down[:, middle:]
    hidden_x = hidden.reshape(nz, groups, nx, units)
    scale_x = scale.reshape(nz, groups, nx, 1)

    def block(offset):
        at = (x_me + offset) % nx
        return (
            lax.dynamic_index_in_dim(hidden_x, at, 2, keepdims=False).swapaxes(0, 1).reshape(rows_z, units),
            lax.dynamic_index_in_dim(scale_x, at, 2, keepdims=False).swapaxes(0, 1).reshape(rows_z, 1),
        )

    h_far, s_far = block(2)
    h_right, s_right = block(1)
    h_left, s_left = block(3)
    h_own, s_own = block(0)

    def part(h, s, weights, more=0.0):
        return (dot(h, weights) * s + more).astype(jnp.bfloat16)

    low_in = lax.ppermute(part(h_far, s_far, down_low), "x", to_right)
    high_in = lax.ppermute(part(h_far, s_far, down_high), "x", to_left)
    left_high_in = lax.ppermute(part(h_right, s_right, down_high), "x", to_right)
    right_low_in = lax.ppermute(part(h_left, s_left, down_low), "x", to_left)
    left_low_in = lax.ppermute(part(h_right, s_right, down_low, low_in), "x", to_right)
    right_high_in = lax.ppermute(part(h_left, s_left, down_high, high_in), "x", to_left)
    back_out = jnp.concatenate(
        [
            part(h_own, s_own, down_low, left_low_in.astype(jnp.float32) + right_low_in),
            part(h_own, s_own, down_high, left_high_in.astype(jnp.float32) + right_high_in),
        ],
        axis=1,
    )
    back_group = lax.all_to_all(back_out, "group", split_axis=0, concat_axis=0, tiled=True)
    back_tokens = jnp.einsum(
        "rt,rd->td", place, back_group, preferred_element_type=jnp.float32
    ).astype(jnp.bfloat16)
    back_parts = lax.all_to_all(back_tokens, "z", split_axis=0, concat_axis=0, tiled=True)
    back_home = jnp.sum(back_parts.reshape(nz, tok_rows, out_width), axis=0, dtype=jnp.float32)
    front_home = lax.all_to_all(
        front_z, ("group", "x"), split_axis=0, concat_axis=0, tiled=True
    )
    result = jnp.concatenate(
        [dot(jnp.repeat(chosen, nx, axis=1), front_home), back_home], axis=1
    )
    return result.astype(jnp.bfloat16)


def solution(mesh):
    groups, columns = mesh.devices.shape
    fine = Mesh(
        mesh.devices.reshape(groups, X_CHIPS, columns // X_CHIPS), ("group", "x", "z")
    )
    lead = ("group", "x", "z")
    in_specs = (
        P(lead, None),
        P(lead, None),
        P(lead, None),
        P(lead, None, None),
        P(lead, None, None),
        P(lead, None, None),
    )
    return jax.shard_map(
        on_device, mesh=fine, in_specs=in_specs, out_specs=P(lead, None), check_vma=False
    )
```

```python
import jax
import jax.numpy as jnp
from jax import lax
from jax.experimental import pallas as pl
from jax.experimental.pallas import tpu as pltpu
from jax.sharding import Mesh, PartitionSpec as P

EXP_GROUP = 8
LANES = 128
X_CHIPS = 4
FRONT = 2304
FRONT_OUT = 2816


ROWS = 128


def expert_kernel(front_ref, both_ref, act_ref, own_ref, down_ref, hidden_ref, out_ref):
    units = hidden_ref.shape[1]
    act = act_ref[...] + jnp.dot(
        front_ref[:, :FRONT], both_ref[...], preferred_element_type=jnp.float32
    )
    gate_act, up_act = act[:, :units], act[:, units:]
    hidden = (gate_act / (1.0 + jnp.exp(-gate_act)) * up_act).astype(jnp.bfloat16)
    hidden_ref[...] = hidden
    table = front_ref[:, FRONT:].astype(jnp.float32)
    scale = jnp.sum(table * own_ref[...], axis=1, keepdims=True)
    out = jnp.dot(hidden, down_ref[...], preferred_element_type=jnp.float32)
    out_ref[...] = (out * scale).astype(jnp.bfloat16)


def expert_rows(front, both, act, own, down):
    rows = front.shape[0]
    units = down.shape[0]

    def by_rows(width):
        return pl.BlockSpec((ROWS, width), lambda i: (i, 0))

    def whole(array):
        return pl.BlockSpec(array.shape, lambda i: (0, 0))

    return pl.pallas_call(
        expert_kernel,
        grid=(rows // ROWS,),
        in_specs=[by_rows(front.shape[1]), whole(both), by_rows(2 * units), whole(own), whole(down)],
        out_specs=[by_rows(units), by_rows(down.shape[1])],
        out_shape=[
            jax.ShapeDtypeStruct((rows, units), jnp.bfloat16),
            jax.ShapeDtypeStruct((rows, down.shape[1]), jnp.bfloat16),
        ],
        compiler_params=pltpu.CompilerParams(vmem_limit_bytes=56 * 1024 * 1024),
        cost_estimate=pl.CostEstimate(
            flops=2 * rows * (2 * both.shape[0] + down.shape[1]) * units,
            bytes_accessed=2 * rows * (front.shape[1] + down.shape[1]),
            transcendentals=rows * units,
        ),
    )(front, both, act, own, down)


def on_device(tokens, expert_ids, gates, gate_weight, up_weight, down_weight):
    groups = lax.axis_size("group")
    nx = lax.axis_size("x")
    nz = lax.axis_size("z")
    slices = nx * nz // EXP_GROUP
    features = tokens.shape[1]
    units = gate_weight.shape[2]
    x_me = lax.axis_index("x")
    to_right = [(i, (i + 1) % nx) for i in range(nx)]
    to_left = [(i, (i - 1) % nx) for i in range(nx)]

    group_of = expert_ids // EXP_GROUP
    local_of = expert_ids % EXP_GROUP
    group_hit = (
        group_of[:, :, None] == jnp.arange(groups, dtype=jnp.int32)[None, None, :]
    ).astype(jnp.float32)
    local_hit = (
        local_of[:, :, None] == jnp.arange(EXP_GROUP, dtype=jnp.int32)[None, None, :]
    ).astype(jnp.float32)
    chosen = (jnp.sum(group_hit, axis=1) > 0).astype(jnp.bfloat16)
    send_rows = jnp.einsum(
        "tg,td->gd", chosen, tokens, preferred_element_type=jnp.float32
    ).astype(jnp.bfloat16)
    weighted_hit = local_hit * gates.astype(jnp.float32)[:, :, None]
    gate_table = jnp.sum(
        group_hit[:, :, :, None] * weighted_hit[:, :, None, :], axis=(0, 1)
    ).astype(jnp.bfloat16)
    width = features - FRONT
    half = width // 2
    front_row = jnp.concatenate(
        [send_rows[:, :FRONT], jnp.pad(gate_table, ((0, 0), (0, LANES - EXP_GROUP)))], axis=1
    )

    back_row = jnp.concatenate(
        [tokens[:, FRONT:], jnp.pad(chosen, ((0, 0), (0, LANES - groups)))], axis=1
    )
    front_send = jnp.broadcast_to(front_row[:, None], (groups, nx, FRONT + LANES)).reshape(
        groups * nx, FRONT + LANES
    )
    copies = jnp.broadcast_to(back_row[None], (nz,) + back_row.shape).reshape(
        nz * back_row.shape[0], back_row.shape[1]
    )
    column = lax.all_to_all(copies, "z", split_axis=0, concat_axis=0, tiled=True)
    front_send, column = lax.optimization_barrier((front_send, column))
    front = lax.all_to_all(
        front_send,
        ("group", "x"),
        split_axis=0,
        concat_axis=0,
        tiled=True,
    )
    front_all = lax.all_gather(front, "z", axis=0, tiled=True)
    tok_rows = tokens.shape[0]
    same_z = (
        jnp.arange(nz, dtype=jnp.int32)[:, None]
        == jnp.arange(nz * tok_rows, dtype=jnp.int32)[None, :] // tok_rows
    ).astype(jnp.bfloat16)
    place = (column[:, width : width + groups].T[:, None, :] * same_z[None]).reshape(
        groups * nz, nz * tok_rows
    )
    back = jnp.dot(place, column[:, :width], preferred_element_type=jnp.float32).astype(
        jnp.bfloat16
    )
    back_own = lax.all_to_all(back, "group", split_axis=0, concat_axis=0, tiled=True)
    own_low, own_high = back_own[:, :half], back_own[:, half:]
    left_low = lax.ppermute(own_low, "x", to_right)
    right_high = lax.ppermute(own_high, "x", to_left)
    left_high = lax.ppermute(own_high, "x", to_right)
    right_low = lax.ppermute(own_low, "x", to_left)
    far_low = lax.ppermute(left_low, "x", to_right)
    far_high = lax.ppermute(right_high, "x", to_left)

    both = jnp.concatenate([gate_weight[0], up_weight[0]], axis=1)
    both_front, both_back = both[:FRONT], both[FRONT:]
    back_low, back_high = both_back[:half], both_back[half:]

    def dot(a, b):
        return jnp.dot(a, b, preferred_element_type=jnp.float32)

    rows_z = back_own.shape[0]
    by_offset = jnp.stack(
        [
            dot(back_own, both_back),
            dot(right_low, back_low) + dot(right_high, back_high),
            dot(far_low, back_low) + dot(far_high, back_high),
            dot(left_low, back_low) + dot(left_high, back_high),
        ]
    ).reshape(nx, groups, nz, 2 * units)
    act_back = jnp.stack(
        [
            lax.dynamic_index_in_dim(by_offset, (x - x_me + nx) % nx, 0, keepdims=False)
            for x in range(nx)
        ],
        axis=2,
    ).transpose(1, 0, 2, 3).reshape(nz * groups * nx, 2 * units)
    mine = (x_me * nz + lax.axis_index("z")) // slices
    own = (jnp.arange(LANES, dtype=jnp.int32) == mine).astype(jnp.float32)
    scale = jnp.sum(front_all[:, FRONT:].astype(jnp.float32) * own[None, :], axis=1, keepdims=True)

    down = down_weight[0]
    hidden, front_out = expert_rows(
        front_all, both_front, act_back, own[None, :], down[:, :FRONT_OUT]
    )
    front_z = lax.psum_scatter(front_out, "z", scatter_dimension=0, tiled=True)
    out_width = features - FRONT_OUT
    middle = FRONT_OUT + out_width // 2
    down_low, down_high = down[:, FRONT_OUT:middle], down[:, middle:]
    hidden_x = hidden.reshape(nz, groups, nx, units)
    scale_x = scale.reshape(nz, groups, nx, 1)

    def block(offset):
        at = (x_me + offset) % nx
        return (
            lax.dynamic_index_in_dim(hidden_x, at, 2, keepdims=False).swapaxes(0, 1).reshape(rows_z, units),
            lax.dynamic_index_in_dim(scale_x, at, 2, keepdims=False).swapaxes(0, 1).reshape(rows_z, 1),
        )

    h_far, s_far = block(2)
    h_right, s_right = block(1)
    h_left, s_left = block(3)
    h_own, s_own = block(0)

    def part(h, s, weights, more=0.0):
        return (dot(h, weights) * s + more).astype(jnp.bfloat16)

    low_in = lax.ppermute(part(h_far, s_far, down_low), "x", to_right)
    high_in = lax.ppermute(part(h_far, s_far, down_high), "x", to_left)
    left_high_in = lax.ppermute(part(h_right, s_right, down_high), "x", to_right)
    right_low_in = lax.ppermute(part(h_left, s_left, down_low), "x", to_left)
    left_low_in = lax.ppermute(part(h_right, s_right, down_low, low_in), "x", to_right)
    right_high_in = lax.ppermute(part(h_left, s_left, down_high, high_in), "x", to_left)
    back_out = jnp.concatenate(
        [
            part(h_own, s_own, down_low, left_low_in.astype(jnp.float32) + right_low_in),
            part(h_own, s_own, down_high, left_high_in.astype(jnp.float32) + right_high_in),
        ],
        axis=1,
    )
    back_group = lax.all_to_all(back_out, "group", split_axis=0, concat_axis=0, tiled=True)
    back_tokens = jnp.einsum(
        "rt,rd->td", place, back_group, preferred_element_type=jnp.float32
    ).astype(jnp.bfloat16)
    back_parts = lax.all_to_all(back_tokens, "z", split_axis=0, concat_axis=0, tiled=True)
    back_home = jnp.sum(back_parts.reshape(nz, tok_rows, out_width), axis=0, dtype=jnp.float32)
    front_home = lax.all_to_all(
        front_z, ("group", "x"), split_axis=0, concat_axis=0, tiled=True
    )
    result = jnp.concatenate(
        [dot(jnp.repeat(chosen, nx, axis=1), front_home), back_home], axis=1
    )
    return result.astype(jnp.bfloat16)


def solution(mesh):
    groups, columns = mesh.devices.shape
    fine = Mesh(
        mesh.devices.reshape(groups, X_CHIPS, columns // X_CHIPS), ("group", "x", "z")
    )
    lead = ("group", "x", "z")
    in_specs = (
        P(lead, None),
        P(lead, None),
        P(lead, None),
        P(lead, None, None),
        P(lead, None, None),
        P(lead, None, None),
    )
    return jax.shard_map(
        on_device, mesh=fine, in_specs=in_specs, out_specs=P(lead, None), check_vma=False
    )
```
